768 devices in a mesh: grp: 16 (over y, core), mem: 48 (over z, x).
Axes of the slice: x: 4, y: 8, z: 12, core: 2. Of those that a mesh axis runs over, the one named last changes fastest.
Arguments:
- points: float32 [196608, 1024], P(('grp', 'mem')), may hold values from -6 to 6
- owner: int32 [196608, 1], P(('grp', 'mem')), may hold values from 0 to 47; in each aligned block of 256 rows (0 to 255, 256 to 511, ...) at most 16 rows name the same one
- slot: int32 [196608], P(('grp', 'mem')), may hold values from 0 to 511
- centroids1: bfloat16 [393216, 1024], P(('grp', 'mem')), may hold values from -6 to 6
- mass1: float32 [393216], P(('grp', 'mem')), may hold values from 0.5 to 16
- parent1: int32 [393216], P(('grp', 'mem')), may hold values from 0 to 767
- centroids2: float32 [768, 1024], P('mem'), may hold values from -6 to 6
- mass2: float32 [768], P('mem'), may hold values from 32 to 1024
- parent2: int32 [768], P('mem'), may hold values from 0 to 255
- centroids3: float32 [256, 1024], replicated, may hold values from -6 to 6
- mass3: float32 [256], replicated, may hold values from 64 to 4096
Outputs:
- new1: bfloat16 [393216, 1024], P(('grp', 'mem'))
- new2: float32 [768, 1024], P('mem')
- new3: float32 [256, 1024], replicated
The draws below stay inside these ranges and needn't reach their ends.
Inputs may be any that keep to these rules, and one draw needn't show every extreme that they name: Among the points of one device at most 16 name the same owner, and in every draw some device has exactly 16 points naming one owner.
All inputs are finite; a program needn't handle non-finite values.
Results may differ from the reference program's by a relative error of at most 0.004.
Values may be sent and summed in bfloat16 or wider, within the bound.
No kernel may reach another device: no remote copies, remote signals or barrier semaphores. Data moves between devices by JAX's collectives and lax.ppermute only.
A program may use at most 32 MiB of HBM per device.

```python
import math
import jax
import jax.numpy as jnp
import numpy as np
from jax import lax

D = 1024
P_DEV = 256
C1_DEV = 512
C3 = 256
CAP = 16
POINTS = 196608
C1 = 393216
C2 = 768
N_GRP = 16
N_MEM = 48


def with_ends(values, rng, least, top_value):
    longest = values.shape.index(max(values.shape))
    spots = []
    for shift in (0, 1):
        where = [jax.random.randint(jax.random.fold_in(rng, axis), (), 0, length) for axis, length in enumerate(values.shape)]
        where[longest] = (where[longest] + shift) % values.shape[longest]
        spots.append(tuple(where))
    return values.at[spots[0]].set(least).at[spots[1]].set(top_value)


def level_of(rng, dims, shards, smallest, largest):
    def one(position, blocks):
        draws = jax.random.uniform(jax.random.fold_in(jax.random.fold_in(rng, 6), position), (blocks,), jnp.float32, smallest / len(shards), largest / len(shards))
        return jnp.repeat(jnp.exp(draws), dims[position] // blocks).reshape((-1,) + (1,) * (len(dims) - position - 1))

    level = one(*shards[0])
    for cut in shards[1:]:
        level = level * one(*cut)
    return level


def rank_table(count, lean):
    weights = [(1 << 20) // math.isqrt(grade ** lean) + 1 for grade in range(1, count + 1)]
    spread = 1 + sum(weights) // (1 << 30)
    return np.cumsum(np.array([max(1, weight // spread) for weight in weights]))


def skewed_ids(rng, shape, count, slope):
    table = rank_table(count, slope)
    pick = jax.random.randint(jax.random.fold_in(rng, 1), shape, 0, int(table[count - 1]))
    grade = jnp.searchsorted(jnp.asarray(table, jnp.int32), pick, side="right")
    return jax.random.permutation(jax.random.fold_in(rng, 2), count)[grade].astype(jnp.int32)


def shared_out(stream_key, own, number, rows, count, top, most, skew):
    ranking = jax.random.permutation(stream_key, count)
    crowded, usual = portions_of(count, rows * top, most, skew, True), portions_of(count, rows * top, most, skew, False)
    places = jnp.arange(count)

    def named(lengths, turn):
        used = int((lengths > 0).sum())
        fixed = max(1, used // 4)
        passed = fixed + (places - fixed + turn * (used - fixed)) % max(1, count - fixed)
        return jnp.zeros((count,), jnp.int32).at[ranking[jnp.where(places < fixed, places, passed)]].set(jnp.asarray(lengths, jnp.int32))

    lengths = jnp.where(number % 4 == 0, named(crowded, number // 4), named(usual, number - number // 4 - 1))
    mixed = jax.random.permutation(jax.random.fold_in(own, 3), count)
    giver, sink = mixed[0:count // 2 * 2:2], mixed[1:count // 2 * 2:2]
    room = jnp.minimum(lengths[giver] - 1, most - lengths[sink]) // 2
    room = jnp.where((giver == ranking[0]) | (sink == ranking[0]) | (lengths[sink] == 0), 0, jnp.maximum(room, 0))
    passed = jax.random.randint(jax.random.fold_in(own, 4), (count // 2,), 0, 1 << 20) % (room + 1)
    lengths = lengths.at[giver].add(-passed).at[sink].add(passed)
    items = jnp.searchsorted(jnp.cumsum(lengths), jnp.arange(rows * top), side="right").astype(jnp.int32)
    table = items.reshape(top, rows).T
    table = table[jax.random.permutation(jax.random.fold_in(own, 1), rows)]
    turn = jax.random.randint(jax.random.fold_in(own, 2), (rows, 1), 0, top)
    return jnp.take_along_axis(table, (jnp.arange(top)[None, :] + turn) % top, axis=1)


def portions_of(amount, total, most, skew, full):
    weights = [(1 << 20) // math.isqrt(rank ** skew) + 1 for rank in range(1, amount + 1)]
    largest = most if full else min(most, max(-(-total // amount), total * weights[0] // sum(weights)))
    least = 1 if total - largest >= amount - 1 else 0
    given, surplus = [largest] + [least] * (amount - 1), total - largest - least * (amount - 1)
    while surplus > 0:
        free = [i for i in range(1, amount) if given[i] < largest] or [i for i in range(1, amount) if given[i] < most]
        whole, left = sum([weights[i] for i in free]), surplus
        for i in free:
            extra = min(most - given[i], max(1, left * weights[i] // whole), surplus)
            given[i] = given[i] + extra
            surplus = surplus - extra
    return np.array(given)


def scatter_about(stream_key, shape, deviation, limit, cuts=(), dtype=jnp.bfloat16):
    array = deviation * jax.random.normal(stream_key, shape, jnp.float32)
    if cuts:
        array = array * level_of(stream_key, shape, cuts, -0.22, 0.18)
    return jnp.clip(array, -limit, limit).astype(dtype)


def setup_inputs(seed: int = 0) -> dict:
    splits = jax.random.split(jax.random.key(seed), 12)
    points = scatter_about(splits[0], (POINTS, D), 1.0, 6.0, ((0, 768),), jnp.float32)
    owner_keys = jax.random.split(jax.random.fold_in(splits[1], 1), POINTS // P_DEV)
    owner_turns = jax.random.permutation(jax.random.fold_in(splits[1], 3), POINTS // P_DEV)
    owner = jax.vmap(lambda own, number: shared_out(jax.random.fold_in(splits[1], 2), own, number, P_DEV, N_MEM, 1, CAP, 2))(owner_keys, owner_turns).reshape((POINTS, 1))
    slot = with_ends(skewed_ids(splits[2], (POINTS,), C1_DEV, 1), jax.random.fold_in(splits[2], 3), 0, C1_DEV - 1).astype(jnp.int32)
    centroids1 = scatter_about(splits[3], (C1, D), 1.0, 6.0, ((0, 768),))
    mass1 = jnp.clip(jnp.exp(math.log(16.0) - 3.465736 * jax.random.uniform(splits[4], (C1,), jnp.float32) ** level_of(splits[4], (C1,), ((0, 768),), -0.2, 0.2)), 0.5, 16.0)
    parent1 = with_ends(jax.random.randint(splits[5], (C1,), 0, C2), jax.random.fold_in(splits[5], 1), 0, C2 - 1).astype(jnp.int32)
    centroids2 = scatter_about(splits[6], (C2, D), 1.0, 6.0, ((0, 48),), jnp.float32)
    mass2 = jnp.clip(jnp.exp(math.log(1024.0) - 3.465736 * jax.random.uniform(splits[7], (C2,), jnp.float32) ** level_of(splits[7], (C2,), ((0, 48),), -0.2, 0.2)), 32.0, 1024.0)
    parent2 = with_ends(jax.random.randint(splits[8], (C2,), 0, C3), jax.random.fold_in(splits[8], 1), 0, C3 - 1).astype(jnp.int32)
    centroids3 = scatter_about(splits[9], (C3, D), 1.0, 6.0, (), jnp.float32)
    mass3 = jnp.clip(jnp.exp(jax.random.uniform(splits[10], (C3,), jnp.float32, math.log(64.0), math.log(4096.0))), 64.0, 4096.0)
    return dict(points=points, owner=owner, slot=slot, centroids1=centroids1, mass1=mass1, parent1=parent1, centroids2=centroids2, mass2=mass2, parent2=parent2, centroids3=centroids3, mass3=mass3)


def reference(points, owner, slot, centroids1, mass1, parent1, centroids2, mass2, parent2, centroids3, mass3):
    group_rows = P_DEV * N_MEM
    group_cents = C1_DEV * N_MEM
    rounded = lax.optimization_barrier(points.astype(jnp.bfloat16)).astype(jnp.float32)
    local_label = (owner[:, 0] * C1_DEV + slot).astype(jnp.int32)

    def one_group(items):
        xs, labels, olds, masses, parents = items
        sums = jax.ops.segment_sum(xs, labels, group_cents)
        counts = jax.ops.segment_sum(jnp.ones((group_rows,), jnp.float32), labels, group_cents)
        fresh = ((sums + masses[:, None] * olds.astype(jnp.float32)) / (counts + masses)[:, None]).astype(jnp.bfloat16)
        part2 = jax.ops.segment_sum(sums, parents, C2)
        cnt2 = jax.ops.segment_sum(counts, parents, C2)
        return fresh, part2, cnt2

    fresh, parts, cnts = lax.map(one_group, (
        rounded.reshape(N_GRP, group_rows, D),
        local_label.reshape(N_GRP, group_rows),
        centroids1.reshape(N_GRP, group_cents, D),
        mass1.reshape(N_GRP, group_cents),
        parent1.reshape(N_GRP, group_cents)))
    new1 = fresh.reshape(C1, D)
    sums2 = jnp.sum(parts, axis=0)
    count2 = jnp.sum(cnts, axis=0)
    new2 = (sums2 + mass2[:, None] * centroids2) / (count2 + mass2)[:, None]
    sums3 = jax.ops.segment_sum(sums2, parent2, C3)
    count3 = jax.ops.segment_sum(count2, parent2, C3)
    new3 = (sums3 + mass3[:, None] * centroids3) / (count3 + mass3)[:, None]
    return new1, new2, new3
```

```python
import jax
import jax.numpy as jnp
from jax import lax
from jax.experimental import pallas as pl
from jax.experimental.pallas import tpu as pltpu
from jax.sharding import Mesh
from jax.sharding import PartitionSpec as P

BF16, F32, I32 = jnp.bfloat16, jnp.float32, jnp.int32
CORES, XS, LANES, CAP, EXTRA = 2, 4, 128, 16, 16
TILES = CORES * XS
ROOM = 32 * 1024 * 1024
MASKS = (1, 2, 6)


def coded(y):
    return y ^ (((y >> 2) & 1) << 1)


def iota(shape, dim):
    return lax.broadcasted_iota(I32, shape, dim)


def dot(a, b, contract=((1,), (0,))):
    return lax.dot_general(a, b, (contract, ((), ())), preferred_element_type=F32)


def column(row):
    eye = iota((LANES, LANES), 0) == iota((LANES, LANES), 1)
    return jnp.sum(jnp.where(eye, row, 0.0), axis=1, keepdims=True)


def encode(counts):
    whole = counts.astype(I32)
    row = iota((EXTRA, LANES), 0)
    parts = jnp.where(row == 0, whole & 0x7FFF0000, jnp.where(row == 1, whole & 0xFF00, whole & 0xFF))
    return jnp.where(row < 3, parts, 0).astype(F32).astype(BF16)


def decode(tile):
    return jnp.sum(tile[0:3].astype(F32), axis=0, keepdims=True)


def ranks(own, members):
    rows = own.shape[1]
    hit = iota((members, rows), 0) == own
    earlier = (iota((rows, rows), 0) < iota((rows, rows), 1)).astype(BF16)
    before = dot(hit.astype(BF16), earlier)
    return jnp.sum(jnp.where(hit, before, 0.0), axis=0, keepdims=True).astype(I32), hit


def table_kernel(owner, slot, parent1, parent2, table, *scratch):
    held, sems = scratch[:-1], scratch[-1]
    copies = [
        pltpu.make_async_copy(src, dst, sems.at[i])
        for i, (src, dst) in enumerate(zip((owner, slot, parent1, parent2), held))
    ]
    for copy in copies:
        copy.start()
    for copy in copies:
        copy.wait()
    owner, slot, parent1, parent2 = held
    members, rows, per = table.shape[0], owner.shape[1], parent2.shape[1]
    place = slot[...]
    rank, hit = ranks(owner[...], members)
    code = jnp.where(place < 256, place + 1, 255 - place).astype(F32)
    spread = (iota((LANES, rows), 0) == per + rank).astype(BF16)
    codes = dot(jnp.where(hit, code, 0.0).astype(BF16), spread, ((1,), (1,)))
    slots = jnp.where(codes > 0, codes - 1, jnp.where(codes < 0, 255 - codes, -1.0)).astype(I32)
    lines = parent1.shape[0]
    row, lane = iota((8, LANES), 0), iota((8, LANES), 1)
    known = jnp.concatenate([parent1[...], jnp.zeros((8 - lines, LANES), I32)], axis=0)
    level2 = jnp.concatenate([parent2[...], jnp.zeros((1, LANES - per), I32)], axis=1)
    known = jnp.where((row == lines) & (lane < per), level2, known)
    for m in range(members):
        table[m] = jnp.where((row == lines) & (lane >= per), slots[m : m + 1, :], known)


def pack_kernel(points, owner, send, rounded):
    rows, members = points.shape[0], send.shape[0]
    rounded[...] = points[...].astype(BF16)
    own = owner[...]
    rank, _ = ranks(own, members)
    pick = (iota((members * CAP, rows), 0) == own * CAP + rank).astype(BF16)
    for pair in range(TILES // 2):
        moved = dot(pick, rounded[:, pair * 2 * LANES : (pair + 1) * 2 * LANES]).astype(BF16)
        for half in range(2):
            tile = moved[:, half * LANES : (half + 1) * LANES].reshape(members, CAP, LANES)
            start = (2 * pair + half) * CAP
            send[:, start : start + CAP, :] = tile


def look_kernel(at, table, owner, slot, rounded, keep, swap):
    core, x = at[0], at[1]
    rows, members = rounded.shape[0], table.shape[0]
    lines = rows // LANES
    hit = (iota((members, rows), 0) == owner[...]).astype(BF16)
    parent = jnp.zeros((1, rows), F32)
    for j in range(4):
        known = table[:, j, :]
        high = (known >> 8).astype(F32).astype(BF16)
        low = (known & 255).astype(F32).astype(BF16)
        found = dot(high, hit, ((0,), (0,))) * 256.0 + dot(low, hit, ((0,), (0,)))
        here = iota((LANES, rows), 0) + j * LANES == slot[...]
        parent += jnp.sum(jnp.where(here, found, 0.0), axis=0, keepdims=True)
    whole = parent.astype(I32)
    parts = [v[:, i * LANES : (i + 1) * LANES] for v in (whole >> 8, whole & 255) for i in range(lines)]
    notes = jnp.zeros((EXTRA, LANES), I32)
    for i, v in enumerate(parts):
        notes = jnp.where(iota((EXTRA, LANES), 0) == i, v, notes)
    notes = notes.astype(F32).astype(BF16)
    for out, to in ((keep, core), (swap, 1 - core)):
        for k in range(XS):
            start = pl.multiple_of((to * XS + ((x + k) & (XS - 1))) * LANES, LANES)
            out[k, 0:rows, :] = rounded[:, pl.ds(start, LANES)]
            out[k, rows : rows + EXTRA, :] = notes


def join_kernel(mine, other, *outs):
    for k in range(1, XS):
        outs[k - 1][0] = mine[k]
        outs[k - 1][1] = other[k]


def part_kernel(at, *refs):
    blocks, (keep, send, total) = refs[:-3], refs[-3:]
    rows = blocks[0].shape[1] - EXTRA
    lines = rows // LANES
    cents = total.shape[0]
    per_y = keep.shape[1] - EXTRA
    ones = jnp.ones((rows, LANES), BF16)
    for s in range(TILES):
        block = blocks[s].at[0] if s < 2 else blocks[2 + (s - 2) // 2].at[s % 2]
        notes = block[rows : rows + EXTRA, :].astype(F32)
        parent = jnp.concatenate(
            [notes[i : i + 1] * 256.0 + notes[lines + i : lines + i + 1] for i in range(lines)], axis=1
        ).astype(I32)
        pick = (iota((cents, rows), 0) == parent).astype(BF16)
        part = dot(pick, jnp.concatenate([block[0:rows, :], ones], axis=1))
        if s == 0:
            total[...] = part
        else:
            total[...] += part
    diagonal = iota((per_y, LANES), 0) == iota((per_y, LANES), 1)
    for i in range(keep.shape[0]):
        for out, bit in ((keep, at[0]), (send, 1 - at[0])):
            start = pl.multiple_of((2 * i + bit) * per_y, 16)
            counts = total[pl.ds(start, per_y), LANES : 2 * LANES]
            row = jnp.sum(jnp.where(diagonal, counts, 0.0), axis=0, keepdims=True)
            out[i, 0:per_y, :] = total[pl.ds(start, per_y), 0:LANES].astype(out.dtype)
            out[i, per_y : per_y + EXTRA, :] = encode(row).astype(out.dtype)


def write(out, i, total):
    per_y = total.shape[0] - EXTRA
    out[i, 0:per_y, :] = total[0:per_y].astype(out.dtype)
    out[i, per_y : per_y + EXTRA, :] = encode(decode(total[per_y:])).astype(out.dtype)


def halve_kernel(at, kept, came, keep, send):
    for i in range(keep.shape[0]):
        for out, bit in ((keep, at[0]), (send, 1 - at[0])):
            j = 2 * i + bit
            write(out, i, kept[j] + came[j].astype(F32))


def last_kernel(kept, came, out):
    write(out, 0, kept[0] + came[0].astype(F32))


def add_kernel(blocks, out):
    total = blocks[0].astype(F32)
    for i in range(1, blocks.shape[0]):
        total = total + blocks[i].astype(F32)
    for i in range(out.shape[0]):
        write(out, i, total)


def level3_kernel(at, held, parents, payload, count3, count2, sums2, counts2):
    z, x = at[0], at[1]
    ys, padded, _ = held.shape
    per_y = padded - EXTRA
    total3 = count3.shape[0]
    sums3 = jnp.zeros((total3, LANES), F32)
    counts3 = jnp.zeros((total3, LANES), F32)
    for y in range(ys):
        block, code = held[y], coded(y)
        row = decode(block[per_y : per_y + EXTRA])
        pick = iota((total3, LANES), 0) == parents[code : code + 1, :]
        counts3 += jnp.where(pick, row, 0.0)
        fill = jnp.zeros((LANES - per_y, LANES), BF16)
        sums3 += dot(
            pick.astype(BF16), jnp.concatenate([block[0:per_y], fill], axis=0)
        )
        sums2[code * per_y : (code + 1) * per_y, :] = block[0:per_y]
        counts2[code * per_y : (code + 1) * per_y, :] = jnp.broadcast_to(
            column(row)[0:per_y], (per_y, LANES)
        )
    count3[...] = jnp.broadcast_to(jnp.sum(counts3, axis=1, keepdims=True), count3.shape)
    start = pl.multiple_of((z * XS + x) * CAP, CAP)
    count2[...] = counts2[pl.ds(start, CAP), :]
    rounded = sums3.astype(BF16)
    for k in range(TILES):
        start = pl.multiple_of((z * XS + k % XS) * CAP, CAP)
        payload[k, 0:total3, :] = rounded
        payload[k, total3 : total3 + CAP, :] = sums2[pl.ds(start, CAP), :]


def top_kernel(held, count3, count2, cents3, mass3, cents2, mass2, new3, new2):
    total3, per = cents3.shape[0], cents2.shape[0]
    weight3 = jnp.concatenate([column(mass3[i : i + 1, :]) for i in range(total3 // LANES)], axis=0)
    weight2 = column(mass2[...])[0:per]
    scale3 = 1.0 / (count3[:, 0:1] + weight3)
    scale2 = 1.0 / (count2[:, 0:1] + weight2)
    for k in range(TILES):
        cols = slice(k * LANES, (k + 1) * LANES)
        new3[:, cols] = (held[k, 0:total3, :].astype(F32) + weight3 * cents3[:, cols]) * scale3
        new2[:, cols] = (
            held[k, total3 : total3 + per, :].astype(F32) + weight2 * cents2[:, cols]
        ) * scale2


def level1_kernel(arrived, place, cents1, mass1, new1):
    members = arrived.shape[0]
    local = cents1.shape[0]
    parts = [
        iota((local, LANES), 0) == place[i : i + 1, :] for i in range(members * CAP // LANES)
    ]
    counts = sum(v.astype(F32) for v in parts)
    counts = jnp.sum(counts, axis=1, keepdims=True)
    pick = jnp.concatenate([v.astype(BF16) for v in parts], axis=1)
    weight = jnp.concatenate([column(mass1[i : i + 1, :]) for i in range(local // LANES)], axis=0)
    scale = 1.0 / (counts + weight)
    for pair in range(TILES // 2):
        halves = [
            arrived[:, t * CAP : (t + 1) * CAP, :].reshape(members * CAP, LANES)
            for t in (2 * pair, 2 * pair + 1)
        ]
        sums = dot(pick, jnp.concatenate(halves, axis=1))
        cols = slice(pair * 2 * LANES, (pair + 1) * 2 * LANES)
        new1[:, cols] = ((sums + weight * cents1[:, cols].astype(F32)) * scale).astype(BF16)


SMEM = pl.BlockSpec(memory_space=pltpu.SMEM)
VMEM = pl.BlockSpec(memory_space=pltpu.VMEM)
HBM = pl.BlockSpec(memory_space=pltpu.HBM)


def call(kernel, outs, args, scalars=0, scratch=(), name=None, places=VMEM, room=ROOM):
    return pl.pallas_call(
        kernel,
        out_shape=outs,
        in_specs=[SMEM] * scalars + [places] * (len(args) - scalars),
        out_specs=jax.tree.map(lambda _: VMEM, outs),
        scratch_shapes=list(scratch),
        compiler_params=pltpu.CompilerParams(vmem_limit_bytes=room),
        name=name,
    )(*args)


def array(shape, dtype=BF16):
    return jax.ShapeDtypeStruct(shape, dtype)


def exchange(v, axes):
    return lax.all_to_all(v, axes, split_axis=0, concat_axis=0, tiled=True)


def local(
    points, owner, slot, centroids1, mass1, parent1, centroids2, mass2, parent2, centroids3, mass3
):
    rows = points.shape[0]
    ys, zs = lax.axis_size("y"), lax.axis_size("z")
    y, core, z, x = (lax.axis_index(a) for a in ("y", "core", "z", "x"))
    members = zs * XS
    per = centroids2.shape[0]
    total2, total3 = per * members, centroids3.shape[0]
    per_y = total2 // ys
    slots = centroids1.shape[0]

    owner, slot = owner.reshape(1, rows), slot.reshape(1, rows)
    small = [owner, slot, parent1.reshape(-1, LANES), parent2.reshape(1, per)]
    table = call(
        table_kernel,
        array((members, 8, LANES), I32),
        small,
        scratch=[pltpu.VMEM(v.shape, I32) for v in small] + [pltpu.SemaphoreType.DMA((len(small),))],
        name="tables",
        places=HBM,
        room=None,
    )
    send, rounded = call(
        pack_kernel,
        [array((members, TILES * CAP, LANES)), array(points.shape)],
        [points, owner],
        name="pack",
    )
    table = exchange(table, ("z", "x"))
    send, table = lax.optimization_barrier((send, table))
    arrived = exchange(send, ("z", "x"))

    kept, other = call(
        look_kernel,
        [array((XS, rows + EXTRA, LANES))] * 2,
        [jnp.stack([core, x]).astype(I32), table, owner, slot, rounded],
        scalars=1,
        name="look_up",
    )
    other = lax.ppermute(other, "core", [(0, 1), (1, 0)])
    joined = call(
        join_kernel, [array((2, rows + EXTRA, LANES))] * (XS - 1), [kept, other], name="join"
    )
    blocks = [kept, other] + [
        lax.ppermute(v, "x", [(i, (i + k) % XS) for i in range(XS)])
        for k, v in enumerate(joined, 1)
    ]

    parents2 = table[:, slots // LANES, 0:per].reshape(ys, per_y)
    parents2 = jnp.pad(parents2, ((0, 0), (0, LANES - per_y)), constant_values=-1)
    places = table[:, slots // LANES, per : per + CAP].reshape(-1, LANES)
    spot = jnp.stack([z, x]).astype(I32)

    def pair(count):
        return [array((count, per_y + EXTRA, LANES), dtype) for dtype in (F32, BF16)]

    count, bit = ys // 2, 0
    kept, going = call(
        part_kernel,
        pair(count),
        [(y & 1).reshape(1).astype(I32), *blocks],
        scalars=1,
        scratch=[pltpu.VMEM((total2, 2 * LANES), F32)],
        name="level2_parts",
    )
    going, parents2, places, spot = lax.optimization_barrier((going, parents2, places, spot))
    while True:
        came = lax.ppermute(going, "y", [(i, i ^ MASKS[bit]) for i in range(ys)])
        if count == 1:
            break
        count, bit = count // 2, bit + 1
        kept, going = call(
            halve_kernel,
            pair(count),
            [((coded(y) >> bit) & 1).reshape(1).astype(I32), kept, came],
            scalars=1,
            name="halve",
        )
    mine = call(
        last_kernel, array((1, per_y + EXTRA, LANES)), [kept, came], name="add_over_y"
    )
    whole = lax.all_gather(mine, "z", tiled=True)
    known = call(
        add_kernel, array((ys, per_y + EXTRA, LANES)), [whole], name="add_over_z"
    )
    known, arrived = lax.optimization_barrier((known, arrived))
    known = exchange(known, "y")

    payload, count3, count2 = call(
        level3_kernel,
        [array((TILES, total3 + CAP, LANES)), array((total3, LANES), F32), array((per, LANES), F32)],
        [spot, known, parents2],
        scalars=1,
        scratch=[pltpu.VMEM((total2, LANES), BF16), pltpu.VMEM((total2, LANES), F32)],
        name="level3_sums",
    )
    payload, arrived = lax.optimization_barrier((payload, arrived))
    payload = exchange(payload, ("core", "x"))
    new3, new2 = call(
        top_kernel,
        [array(centroids3.shape, F32), array(centroids2.shape, F32)],
        [
            payload,
            count3,
            count2,
            centroids3,
            mass3.reshape(-1, LANES),
            centroids2,
            jnp.pad(mass2, (0, LANES - per)).reshape(1, LANES),
        ],
        name="new3_new2",
    )
    new1 = call(
        level1_kernel,
        array(centroids1.shape),
        [arrived, places, centroids1, mass1.reshape(-1, LANES)],
        name="new1",
    )
    return (new1, new2, new3)


def solution(mesh):
    grp, mem = mesh.devices.shape
    shape = (grp // CORES, CORES, mem // XS, XS)
    fine = Mesh(mesh.devices.reshape(shape), ("y", "core", "z", "x"))
    both, zx = P(("y", "core", "z", "x")), P(("z", "x"))
    placed = (both,) * 6 + (zx,) * 3 + (P(),) * 2
    return jax.shard_map(
        local,
        mesh=fine,
        in_specs=placed,
        out_specs=(both, zx, P()),
        check_vma=False,
    )
```
